256 devices in a mesh: rows: 128 (over z, y_lo, x, core), rep: 2 (over y_hi).
Axes of the slice: x: 4, y: 4 (y_hi: 2, y_lo: 2; y = y_hi * 2 + y_lo), z: 8, core: 2. Of those that a mesh axis runs over, the one named last changes fastest.
Arguments:
- features: bfloat16 [65536, 128], P('rows'), may hold values from -6 to 6
- w_first: bfloat16 [128, 512], replicated, may hold values from -0.5 to 0.5
- w_second: bfloat16 [512, 172], replicated, may hold values from -0.25 to 0.25
- adj_blocks: bfloat16 [128, 16, 4, 128, 128], P('rows', 'rep'), may hold values from -0.125 to 0.125
- adj_cols: int32 [128, 16, 4], P('rows', 'rep'), may hold values from 0 to 511, as said below
- train_mask: int32 [65536], P('rows'), may hold values 0 or 1
- cotangent: bfloat16 [65536, 172], P('rows'), may hold values from -0.0234375 to 0.0234375
Outputs:
- logits: bfloat16 [65536, 172], P('rows')
- grad_first: float32 [128, 512], replicated
- grad_second: float32 [512, 172], replicated
The draws below stay inside these ranges and needn't reach their ends.
Inputs may be any that keep to these rules, and one draw needn't show every extreme that they name: `adj_cols`: each tile of panel p lies in a block column of panels p - 1 to p + 1, that is from (p - 1) * 4 to (p + 2) * 4 - 1, within the slab; slot 0 of each block row is its diagonal tile.
All inputs are finite; a program needn't handle non-finite values. No bound on the sum of `train_mask` on one device may be relied on, other than what follows from the above.
Results may differ from the reference program's by a relative error of at most 0.013.
Values may be sent and summed in bfloat16 or wider, within the bound.
No kernel may reach another device: no remote copies, remote signals or barrier semaphores. Data moves between devices by JAX's collectives and lax.ppermute only.
A program may use at most 192 MiB of HBM per device.

```python
import jax
import jax.numpy as jnp
from jax import lax

F = 128
H = 512
C = 172
NODE_DEV = 512
PER_ROW = 16
BR = 4
PANELS = 128
NODES = 65536
NBLOCKS = 512


def draw_adj_cols(key, part):
    key = jax.random.fold_in(key, 7)
    tile_shape = (PANELS, PER_ROW, BR)
    panel_number = jnp.arange(PANELS, dtype=jnp.int32)[:, None, None]
    slot_number = jnp.arange(PER_ROW, dtype=jnp.int32)[None, :, None]
    row_number = jnp.arange(BR, dtype=jnp.int32)[None, None, :]
    offset = jax.random.randint(key, tile_shape, -BR, 2 * BR, dtype=jnp.int32)
    offset = jnp.where(slot_number == 0, row_number, offset)
    offset = jnp.where((slot_number == 1) & (row_number == 0), -BR, offset)
    offset = jnp.where((slot_number == 1) & (row_number == BR - 1), 2 * BR - 1, offset)
    column = panel_number * BR + offset
    outside = (column < 0) | (column >= NBLOCKS)
    column = jnp.where(outside, panel_number * BR + BR - 1 - offset, column)
    return column.astype(jnp.int32)


def touch_ends(drawn, rng, least, high):
    dims = drawn.shape
    index_at = [jax.random.randint(jax.random.fold_in(rng, axis), (), 0, dims[axis]) for axis in range(len(dims))]
    drawn = drawn.at[tuple(index_at)].set(least)
    longest = dims.index(max(dims))
    index_at[longest] = (index_at[longest] + 1) % dims[longest]
    return drawn.at[tuple(index_at)].set(high)


def steps_of(own_key, dims, cuts, smallest, largest):
    gain = 1.0
    for dim, parts in cuts:
        draws = jax.random.uniform(jax.random.fold_in(jax.random.fold_in(own_key, 6), dim), (parts,), jnp.float32, smallest / len(cuts), largest / len(cuts))
        gain = gain * jnp.repeat(jnp.exp(draws), dims[dim] // parts).reshape((-1,) + (1,) * (len(dims) - 1 - dim))
    return gain


def noise(rng, shape, scale, most, shards=(), held_as=jnp.bfloat16):
    drawn = scale * jax.random.normal(rng, shape, jnp.float32)
    if shards:
        drawn = drawn * steps_of(rng, shape, shards, -0.22, 0.18)
    return jnp.clip(drawn, -most, most).astype(held_as)


def setup_inputs(seed: int = 0) -> dict:
    keys = jax.random.split(jax.random.key(seed), 8)
    features = noise(keys[0], (NODES, F), 1.0, 6.0, ((0, 128),))
    w_first = noise(keys[1], (F, H), F ** -0.5, 0.5)
    w_second = noise(keys[2], (H, C), H ** -0.5, 0.25)
    adj_blocks = noise(keys[3], (PANELS, PER_ROW, BR, 128, 128), (128 * PER_ROW) ** -0.5, 0.125, ((0, 128), (1, 2)))
    adj_cols = draw_adj_cols(jax.random.fold_in(keys[7], 71), 0)
    train_mask = touch_ends((jax.random.randint(keys[5], (NODES,), 0, 2) < 1).astype(jnp.int32), jax.random.fold_in(keys[5], 1), 0, 1)
    cotangent = noise(keys[6], (NODES, C), (1.0 / NODES ** 0.5), 0.0234375, ((0, 128),))
    return dict(features=features, w_first=w_first, w_second=w_second, adj_blocks=adj_blocks, adj_cols=adj_cols, train_mask=train_mask, cotangent=cotangent)


def aggregate(table, adj_blocks, adj_cols):
    feat_width = table.shape[1]
    tile_table = table.reshape(NBLOCKS, 128, feat_width)

    def per_panel(operands):
        blocks, columns = operands
        tile_rows = jnp.take(tile_table, columns, axis=0).astype(jnp.float32)
        result = jnp.einsum('krij,krjw->riw', blocks.astype(jnp.float32), tile_rows)
        return result.reshape(NODE_DEV, feat_width)
    return lax.map(per_panel, (adj_blocks, adj_cols)).reshape(NODES, feat_width)

def transpose_aggregate(table, adj_blocks, adj_cols):
    feat_width = table.shape[1]
    grad_tiles = table.reshape(PANELS, BR, 128, feat_width)

    def panel_step(total, operands):
        blocks, columns, tile_part = operands
        contribution = jnp.einsum('krij,riw->krjw', blocks.astype(jnp.float32), tile_part.astype(jnp.float32))
        total = total.at[columns.reshape(-1)].add(contribution.reshape(-1, 128, feat_width))
        return (total, None)
    start = jnp.zeros((NBLOCKS, 128, feat_width), jnp.float32)
    total, unused = lax.scan(panel_step, start, (adj_blocks, adj_cols, grad_tiles))
    return total.reshape(NODES, feat_width)

def reference(features, w_first, w_second, adj_blocks, adj_cols, train_mask, cotangent):
    summed = aggregate(features, adj_blocks, adj_cols).astype(jnp.bfloat16)
    pre_act = jnp.dot(summed, w_first, preferred_element_type=jnp.float32)
    activated, act_back = jax.vjp(jax.nn.gelu, pre_act)
    hidden = activated.astype(jnp.bfloat16)
    projected = jnp.dot(hidden, w_second, preferred_element_type=jnp.float32).astype(jnp.bfloat16)
    logits = aggregate(projected, adj_blocks, adj_cols).astype(jnp.bfloat16)
    masked_grad = cotangent * train_mask[:, None].astype(jnp.bfloat16)
    back_sum = transpose_aggregate(masked_grad, adj_blocks, adj_cols).astype(jnp.bfloat16)
    grad_second = jnp.dot(hidden.T, back_sum, preferred_element_type=jnp.float32)
    hidden_grad = jnp.dot(back_sum, w_second.T, preferred_element_type=jnp.float32)
    pre_grad = act_back(hidden_grad)[0].astype(jnp.bfloat16)
    grad_first = jnp.dot(summed.T, pre_grad, preferred_element_type=jnp.float32)
    return (logits, grad_first, grad_second)
```

```python
import functools

import jax
import jax.numpy as jnp
from jax import lax
from jax.experimental import pallas as pl
from jax.experimental.pallas import tpu as pltpu
from jax.sharding import PartitionSpec as P

BF = jnp.bfloat16
F32 = jnp.float32
TILE = 128
ROOT = 0.7978845608028654
CUBE = 0.044715
VMEM = pl.BlockSpec(memory_space=pltpu.VMEM)
SMEM = pl.BlockSpec(memory_space=pltpu.SMEM)


def dot(a, b, contract):
    return lax.dot_general(a, b, ((contract[:1], contract[1:]), ((), ())), preferred_element_type=F32)


def call(kernel, outs, ins, scratch=(), flops=0, specs=None):
    size = lambda x: x.size * x.dtype.itemsize
    moved = sum(map(size, ins)) + sum(map(size, outs))
    return pl.pallas_call(
        kernel,
        out_shape=outs,
        in_specs=specs or [VMEM] * len(ins),
        out_specs=[VMEM] * len(outs),
        scratch_shapes=list(scratch),
        compiler_params=pltpu.CompilerParams(vmem_limit_bytes=48 * 1024 * 1024),
        cost_estimate=pl.CostEstimate(flops=flops, bytes_accessed=moved, transcendentals=0),
    )(*ins)


def slab_kernel(first_ref, cols_ref, blocks_ref, cot_ref, mask_ref, slab_ref, to_before_ref, own_ref, to_after_ref, acc):
    slots, block_rows = blocks_ref.shape[:2]
    rows = block_rows * TILE
    first = first_ref[0]
    acc[...] = jnp.zeros_like(acc)
    for k in range(slots):
        for r in range(block_rows):
            local = cols_ref[r, k] - first
            where = (pl.ds(r * TILE, TILE), pl.ds(pl.multiple_of(local * TILE, TILE), TILE))
            acc[where] += blocks_ref[k, r].astype(F32)
    grad = cot_ref[...] * mask_ref[...].astype(BF)
    for part, out in enumerate((to_before_ref, own_ref, to_after_ref)):
        columns = pl.ds(part * rows, rows)
        slab = acc[:, columns].astype(BF)
        slab_ref[:, columns] = slab
        out[...] = dot(grad, slab, (1, 0)).astype(out.dtype)


def first_sum_kernel(slab_ref, before_ref, own_ref, after_ref, out_ref):
    rows = slab_ref.shape[0]
    total = dot(slab_ref[:, pl.ds(0, rows)], before_ref[...], (1, 0))
    total += dot(slab_ref[:, pl.ds(rows, rows)], own_ref[...], (1, 0))
    total += dot(slab_ref[:, pl.ds(2 * rows, rows)], after_ref[...], (1, 0))
    out_ref[...] = total.astype(out_ref.dtype)


def hidden_kernel(mine_ref, other_ref, w1_ref, w2_ref, summed_ref, hidden_ref, slope_ref, proj_ref):
    rows = mine_ref.shape[0]
    for start in range(0, rows, TILE):
        here = pl.ds(start, TILE)
        summed = (mine_ref[here, :].astype(F32) + other_ref[here, :].astype(F32)).astype(BF)
        summed_ref[here, :] = summed
        v = dot(summed, w1_ref[...], (1, 0))
        square = v * v
        t = jnp.tanh(ROOT * (v + CUBE * (square * v)))
        half = 0.5 * (1.0 + t)
        hidden = (v * half).astype(BF)
        hidden_ref[here, :] = hidden
        slope_ref[here, :] = half + (0.5 * ROOT) * v * ((1.0 - t) * (1.0 + t)) * (1.0 + (3.0 * CUBE) * square)
        proj_ref[:, here] = dot(w2_ref[...], hidden, (1, 1)).astype(BF)


def grads_kernel(summed_ref, hidden_ref, slope_ref, own_ref, before_ref, after_ref, w2_ref, out_ref):
    feats = summed_ref.shape[1]
    classes = own_ref.shape[0]
    back = (own_ref[...].astype(F32) + before_ref[...].astype(F32) + after_ref[...].astype(F32)).astype(BF)
    second = dot(back, hidden_ref[...], (1, 0))
    hidden_grad = dot(back, w2_ref[...], (0, 0))
    pre_grad = (hidden_grad * slope_ref[...]).astype(BF)
    first = dot(summed_ref[...], pre_grad, (0, 0))
    out_ref[pl.ds(0, feats), :] = first.astype(BF)
    out_ref[pl.ds(feats, classes), :] = second.astype(BF)
    rest = out_ref.shape[0] - feats - classes
    if rest:
        out_ref[pl.ds(feats + classes, rest), :] = jnp.zeros((rest, out_ref.shape[1]), BF)


def logits_kernel(slab_ref, before_ref, own_ref, after_ref, out_ref):
    rows = slab_ref.shape[0]
    total = dot(before_ref[...], slab_ref[:, pl.ds(0, rows)], (1, 1))
    total += dot(own_ref[...], slab_ref[:, pl.ds(rows, rows)], (1, 1))
    total += dot(after_ref[...], slab_ref[:, pl.ds(2 * rows, rows)], (1, 1))
    out_ref[...] = total.astype(out_ref.dtype)


def to_units(x):
    rows, width = x.shape
    x = x.reshape(rows // 8, 4, 2, width // TILE, TILE)
    return x.transpose(0, 3, 1, 2, 4).reshape(-1, 2, TILE)


def from_units(units, width):
    x = units.reshape(-1, width // TILE, 4, 2, TILE)
    return x.transpose(0, 2, 3, 1, 4).reshape(-1, width)


def body(features, w_first, w_second, adj_blocks, adj_cols, train_mask, cotangent):
    panels, reps = lax.axis_size("rows"), lax.axis_size("rep")
    rows, feats = features.shape
    block_rows = adj_cols.shape[2]
    hidden_units, classes = w_second.shape
    up = [(i, (i + 1) % panels) for i in range(panels)]
    down = [(j, i) for i, j in up]
    swap = [(i, (i + 1) % reps) for i in range(reps)]
    shape = jax.ShapeDtypeStruct
    w2 = w_second.T
    cot = cotangent.T

    feats_before = lax.ppermute(features, "rows", up)
    feats_after = lax.ppermute(features, "rows", down)
    first = ((lax.axis_index("rows") - 1) * block_rows).astype(jnp.int32).reshape(1)
    slab, to_before, own, to_after = call(
        slab_kernel,
        [shape((rows, 3 * rows), BF), shape((classes, rows), BF), shape((classes, rows), F32), shape((classes, rows), BF)],
        [first, adj_cols[0].T, adj_blocks[0], cot, train_mask.reshape(1, rows)],
        [pltpu.VMEM((rows, 3 * rows), F32)],
        flops=6 * rows * rows * classes,
        specs=[SMEM, SMEM, VMEM, VMEM, VMEM],
    )
    back_after = lax.ppermute(to_before, "rows", down)
    back_before = lax.ppermute(to_after, "rows", up)

    (mine,) = call(
        first_sum_kernel, [shape((rows, feats), BF)], [slab, feats_before, features, feats_after], flops=6 * rows * rows * feats
    )
    other = lax.ppermute(mine, "rep", swap)
    summed, hidden, slope, proj = call(
        hidden_kernel,
        [shape((rows, feats), BF), shape((rows, hidden_units), BF), shape((rows, hidden_units), F32), shape((classes, rows), BF)],
        [mine, other, w_first, w2],
        flops=2 * rows * hidden_units * (feats + classes),
    )
    proj_before = lax.ppermute(proj, "rows", up)
    proj_after = lax.ppermute(proj, "rows", down)

    devices = panels * reps
    unit_rows = 8 * devices // 4 // (hidden_units // TILE)
    padded = -(-(feats + classes) // unit_rows) * unit_rows
    (grads,) = call(
        grads_kernel,
        [shape((padded, hidden_units), BF)],
        [summed, hidden, slope, own, back_before, back_after, w2],
        flops=2 * rows * hidden_units * (feats + 2 * classes),
    )
    both = ("rows", "rep")
    units = to_units(grads).reshape(devices, -1, 2, TILE)
    parts = lax.all_to_all(units, both, 0, 0)
    part = jnp.sum(parts.astype(F32), axis=0).astype(BF)
    whole = lax.all_to_all(jnp.broadcast_to(part[None], units.shape), both, 0, 0)
    reduced = from_units(whole, hidden_units).astype(F32)
    grad_first = reduced[:feats]
    grad_second = reduced[feats : feats + classes].T

    (mine_logits,) = call(
        logits_kernel, [shape((classes, rows), BF)], [slab, proj_before, proj, proj_after], flops=6 * rows * rows * classes
    )
    other_logits = lax.ppermute(mine_logits, "rep", swap)
    logits = (mine_logits.astype(F32) + other_logits.astype(F32)).astype(BF).T
    return (logits, grad_first, grad_second)


def solution(mesh):
    in_specs = (
        P("rows", None),
        P(),
        P(),
        P("rows", "rep", None, None, None),
        P("rows", "rep", None),
        P("rows"),
        P("rows", None),
    )
    out_specs = (P("rows", None), P(), P())
    return jax.shard_map(body, mesh=mesh, in_specs=in_specs, out_specs=out_specs, check_vma=False)
```

```python
import jax
import jax.numpy as jnp
from jax import lax
from jax.experimental import pallas as pl
from jax.experimental.pallas import tpu as pltpu
from jax.sharding import PartitionSpec as P

BF = jnp.bfloat16
F32 = jnp.float32
TILE = 128
ROOT = 0.7978845608028654
CUBE = 0.044715
VMEM = pl.BlockSpec(memory_space=pltpu.VMEM)
ANY = pl.BlockSpec(memory_space=pl.ANY)
SMEM = pl.BlockSpec(memory_space=pltpu.SMEM)


def dot(a, b, contract):
    return lax.dot_general(a, b, ((contract[:1], contract[1:]), ((), ())), preferred_element_type=F32)


def call(kernel, outs, ins, scratch=(), flops=0, specs=None):
    size = lambda x: x.size * x.dtype.itemsize
    moved = sum(map(size, ins)) + sum(map(size, outs))
    return pl.pallas_call(
        kernel,
        out_shape=outs,
        in_specs=specs or [VMEM] * len(ins),
        out_specs=[VMEM] * len(outs),
        scratch_shapes=list(scratch),
        compiler_params=pltpu.CompilerParams(vmem_limit_bytes=48 * 1024 * 1024),
        cost_estimate=pl.CostEstimate(flops=flops, bytes_accessed=moved, transcendentals=0),
    )(*ins)


def slab_kernel(first_ref, cols_ref, blocks_ref, slab_ref, acc):
    slots, block_rows = blocks_ref.shape[:2]
    first = first_ref[0]
    acc[...] = jnp.zeros_like(acc)
    for k in range(slots):
        for r in range(block_rows):
            local = cols_ref[r, k] - first
            where = (pl.ds(r * TILE, TILE), pl.ds(pl.multiple_of(local * TILE, TILE), TILE))
            acc[where] += blocks_ref[k, r].astype(F32)
    slab_ref[...] = acc[...].astype(BF)


def back_kernel(slab_ref, cot_ref, mask_ref, after_ref, to_before_ref, own_ref, to_after_ref):
    rows = slab_ref.shape[0]
    grad = cot_ref[...] * mask_ref[...].astype(BF)
    for part, out in enumerate((to_before_ref, own_ref, to_after_ref)):
        out[...] = dot(grad, slab_ref[:, pl.ds(part * rows, rows)], (1, 0)).astype(out.dtype)


def first_sum_kernel(slab_ref, before_ref, own_ref, after_ref, out_ref):
    rows = slab_ref.shape[0]
    total = dot(slab_ref[:, pl.ds(0, rows)], before_ref[...], (1, 0))
    total += dot(slab_ref[:, pl.ds(rows, rows)], own_ref[...], (1, 0))
    total += dot(slab_ref[:, pl.ds(2 * rows, rows)], after_ref[...], (1, 0))
    out_ref[...] = total.astype(out_ref.dtype)


def hidden_kernel(mine_ref, other_ref, w1_ref, w2_ref, summed_ref, hidden_ref, slope_ref, proj_ref):
    rows = mine_ref.shape[0]
    for start in range(0, rows, TILE):
        here = pl.ds(start, TILE)
        summed = (mine_ref[here, :].astype(F32) + other_ref[here, :].astype(F32)).astype(BF)
        summed_ref[here, :] = summed
        v = dot(summed, w1_ref[...], (1, 0))
        square = v * v
        t = jnp.tanh(ROOT * (v + CUBE * (square * v)))
        half = 0.5 * (1.0 + t)
        hidden = (v * half).astype(BF)
        hidden_ref[here, :] = hidden
        slope_ref[here, :] = half + (0.5 * ROOT) * v * ((1.0 - t) * (1.0 + t)) * (1.0 + (3.0 * CUBE) * square)
        proj_ref[:, here] = dot(w2_ref[...], hidden, (1, 1)).astype(BF)


def grads_kernel(summed_ref, hidden_ref, slope_ref, own_ref, before_ref, after_ref, w2_ref, out_ref):
    feats = summed_ref.shape[1]
    classes = own_ref.shape[0]
    back = (own_ref[...].astype(F32) + before_ref[...].astype(F32) + after_ref[...].astype(F32)).astype(BF)
    second = dot(back, hidden_ref[...], (1, 0))
    hidden_grad = dot(back, w2_ref[...], (0, 0))
    pre_grad = (hidden_grad * slope_ref[...]).astype(BF)
    first = dot(summed_ref[...], pre_grad, (0, 0))
    out_ref[pl.ds(0, feats), :] = first.astype(BF)
    out_ref[pl.ds(feats, classes), :] = second.astype(BF)
    rest = out_ref.shape[0] - feats - classes
    if rest:
        out_ref[pl.ds(feats + classes, rest), :] = jnp.zeros((rest, out_ref.shape[1]), BF)


def logits_kernel(slab_ref, before_ref, own_ref, after_ref, out_ref):
    rows = slab_ref.shape[0]
    total = dot(before_ref[...], slab_ref[:, pl.ds(0, rows)], (1, 1))
    total += dot(own_ref[...], slab_ref[:, pl.ds(rows, rows)], (1, 1))
    total += dot(after_ref[...], slab_ref[:, pl.ds(2 * rows, rows)], (1, 1))
    out_ref[...] = total.astype(out_ref.dtype)


def sum_kernel(parts_ref, out_ref):
    total = parts_ref[0].astype(F32)
    for i in range(1, parts_ref.shape[0]):
        total += parts_ref[i].astype(F32)
    total = total.astype(BF)
    for i in range(out_ref.shape[0]):
        out_ref[i] = total


def unpack_kernel(whole_ref, first_ref, second_ref):
    feats, classes = first_ref.shape[0], second_ref.shape[0]
    first_ref[...] = whole_ref[pl.ds(0, feats), :].astype(F32)
    second_ref[...] = whole_ref[pl.ds(feats, classes), :].astype(F32)


def to_chunks(x, chunks):
    rows, width = x.shape
    return x.reshape(rows // 8, 8, width // TILE, TILE).transpose(0, 2, 1, 3).reshape(chunks, -1, TILE)


def from_chunks(x, width):
    return x.reshape(-1, width // TILE, 8, TILE).transpose(0, 2, 1, 3).reshape(-1, width)


def summed_everywhere(x):
    panels, reps = lax.axis_size("rows"), lax.axis_size("rep")
    devices, layers = panels * reps, 8
    plane = devices // layers
    planes = [[b * plane + i for i in range(plane)] for b in range(layers)]
    columns = [[b * plane + i for b in range(layers)] for i in range(plane)]
    exchange = lambda v, groups: lax.all_to_all(v, ("rows", "rep"), 0, 0, axis_index_groups=groups)
    chunks = to_chunks(x, plane)
    chunk = chunks.shape[1:]
    (copies,) = call(sum_kernel, [jax.ShapeDtypeStruct((layers, *chunk), BF)], [exchange(chunks, planes)])
    (copies,) = call(sum_kernel, [jax.ShapeDtypeStruct((plane, *chunk), BF)], [exchange(copies, columns)])
    return from_chunks(exchange(copies, planes), x.shape[1])


def body(features, w_first, w_second, adj_blocks, adj_cols, train_mask, cotangent):
    panels, reps = lax.axis_size("rows"), lax.axis_size("rep")
    rows, feats = features.shape
    block_rows = adj_cols.shape[2]
    hidden_units, classes = w_second.shape
    up = [(i, (i + 1) % panels) for i in range(panels)]
    down = [(j, i) for i, j in up]
    swap = [(i, (i + 1) % reps) for i in range(reps)]
    shape = jax.ShapeDtypeStruct
    w2 = w_second.T
    cot = cotangent.T

    feats_before = lax.ppermute(features, "rows", up)
    feats_after = lax.ppermute(features, "rows", down)
    first = ((lax.axis_index("rows") - 1) * block_rows).astype(jnp.int32).reshape(1)
    (slab,) = call(
        slab_kernel,
        [shape((rows, 3 * rows), BF)],
        [first, adj_cols[0].T, adj_blocks[0]],
        [pltpu.VMEM((rows, 3 * rows), F32)],
        flops=6 * rows * rows,
        specs=[SMEM, SMEM, VMEM],
    )

    (mine,) = call(
        first_sum_kernel, [shape((rows, feats), BF)], [slab, feats_before, features, feats_after], flops=6 * rows * rows * feats
    )
    other = lax.ppermute(mine, "rep", swap)
    to_before, own, to_after = call(
        back_kernel,
        [shape((classes, rows), BF), shape((classes, rows), F32), shape((classes, rows), BF)],
        [slab, cot, train_mask.reshape(1, rows), mine],
        flops=6 * rows * rows * classes,
        specs=[VMEM, VMEM, VMEM, ANY],
    )
    back_after = lax.ppermute(to_before, "rows", down)
    back_before = lax.ppermute(to_after, "rows", up)
    summed, hidden, slope, proj = call(
        hidden_kernel,
        [shape((rows, feats), BF), shape((rows, hidden_units), BF), shape((rows, hidden_units), F32), shape((classes, rows), BF)],
        [mine, other, w_first, w2],
        flops=2 * rows * hidden_units * (feats + classes),
    )
    proj_before = lax.ppermute(proj, "rows", up)
    proj_after = lax.ppermute(proj, "rows", down)

    tile_rows = 8 * 8
    padded = -(-(feats + classes) // tile_rows) * tile_rows
    (grads,) = call(
        grads_kernel,
        [shape((padded, hidden_units), BF)],
        [summed, hidden, slope, own, back_before, back_after, w2],
        flops=2 * rows * hidden_units * (feats + 2 * classes),
    )
    grad_first, grad_second = call(
        unpack_kernel, [shape((feats, hidden_units), F32), shape((classes, hidden_units), F32)], [summed_everywhere(grads)]
    )
    grad_second = grad_second.T

    (mine_logits,) = call(
        logits_kernel, [shape((classes, rows), BF)], [slab, proj_before, proj, proj_after], flops=6 * rows * rows * classes
    )
    other_logits = lax.ppermute(mine_logits, "rep", swap)
    logits = (mine_logits.astype(F32) + other_logits.astype(F32)).astype(BF).T
    return (logits, grad_first, grad_second)


def solution(mesh):
    in_specs = (
        P("rows", None),
        P(),
        P(),
        P("rows", "rep", None, None, None),
        P("rows", "rep", None),
        P("rows"),
        P("rows", None),
    )
    out_specs = (P("rows", None), P(), P())
    return jax.shard_map(body, mesh=mesh, in_specs=in_specs, out_specs=out_specs, check_vma=False)
```

```python
import jax
import jax.numpy as jnp
from jax import lax
from jax.experimental import pallas as pl
from jax.experimental.pallas import tpu as pltpu
from jax.sharding import PartitionSpec as P

BF = jnp.bfloat16
F32 = jnp.float32
TILE = 128
ROOT = 0.7978845608028654
CUBE = 0.044715
VMEM = pl.BlockSpec(memory_space=pltpu.VMEM)
ANY = pl.BlockSpec(memory_space=pl.ANY)
SMEM = pl.BlockSpec(memory_space=pltpu.SMEM)


def dot(a, b, contract):
    return lax.dot_general(a, b, ((contract[:1], contract[1:]), ((), ())), preferred_element_type=F32)


def call(kernel, outs, ins, scratch=(), flops=0, specs=None, vmem=48 * 2**20):
    size = lambda x: x.size * x.dtype.itemsize
    moved = sum(map(size, ins)) + sum(map(size, outs))
    return pl.pallas_call(
        kernel,
        out_shape=outs,
        in_specs=specs or [VMEM] * len(ins),
        out_specs=[VMEM] * len(outs),
        scratch_shapes=list(scratch),
        compiler_params=pltpu.CompilerParams(vmem_limit_bytes=vmem),
        cost_estimate=pl.CostEstimate(flops=flops, bytes_accessed=moved, transcendentals=0),
    )(*ins)


def slab_kernel(first_ref, cols_hbm, blocks_hbm, slab_ref, acc, cols_ref, blocks_ref, sems):
    slots, block_rows = blocks_ref.shape[:2]
    copies = [pltpu.make_async_copy(cols_hbm, cols_ref, sems.at[slots])]
    copies += [pltpu.make_async_copy(blocks_hbm.at[k], blocks_ref.at[k], sems.at[k]) for k in range(slots)]
    for copy in copies:
        copy.start()
    first = first_ref[0]
    acc[...] = jnp.zeros_like(acc)
    copies[0].wait()
    for k in range(slots):
        copies[1 + k].wait()
        for r in range(block_rows):
            local = cols_ref[r, k] - first
            where = (pl.ds(r * TILE, TILE), pl.ds(pl.multiple_of(local * TILE, TILE), TILE))
            acc[where] += blocks_ref[k, r].astype(F32)
    slab_ref[...] = acc[...].astype(BF)


def back_kernel(slab_ref, cot_ref, mask_ref, after_ref, to_before_ref, own_ref, to_after_ref):
    rows = slab_ref.shape[0]
    grad = cot_ref[...] * mask_ref[...].astype(BF)
    for part, out in enumerate((to_before_ref, own_ref, to_after_ref)):
        out[...] = dot(grad, slab_ref[:, pl.ds(part * rows, rows)], (1, 0)).astype(out.dtype)


def first_sum_kernel(slab_ref, before_ref, own_ref, after_ref, out_ref):
    rows = slab_ref.shape[0]
    total = dot(slab_ref[:, pl.ds(0, rows)], before_ref[...], (1, 0))
    total += dot(slab_ref[:, pl.ds(rows, rows)], own_ref[...], (1, 0))
    total += dot(slab_ref[:, pl.ds(2 * rows, rows)], after_ref[...], (1, 0))
    out_ref[...] = total.astype(out_ref.dtype)


def hidden_kernel(mine_ref, other_ref, w1_ref, w2_ref, summed_ref, hidden_ref, slope_ref, proj_ref):
    rows = mine_ref.shape[0]
    for start in range(0, rows, TILE):
        here = pl.ds(start, TILE)
        summed = (mine_ref[here, :].astype(F32) + other_ref[here, :].astype(F32)).astype(BF)
        summed_ref[here, :] = summed
        v = dot(summed, w1_ref[...], (1, 0))
        square = v * v
        t = jnp.tanh(ROOT * (v + CUBE * (square * v)))
        half = 0.5 * (1.0 + t)
        hidden = (v * half).astype(BF)
        hidden_ref[here, :] = hidden
        slope_ref[here, :] = half + (0.5 * ROOT) * v * ((1.0 - t) * (1.0 + t)) * (1.0 + (3.0 * CUBE) * square)
        proj_ref[:, here] = dot(w2_ref[...], hidden, (1, 1)).astype(BF)


def grads_kernel(summed_ref, hidden_ref, slope_ref, own_ref, before_ref, after_ref, w2_ref, out_ref):
    feats = summed_ref.shape[1]
    classes = own_ref.shape[0]
    back = (own_ref[...].astype(F32) + before_ref[...].astype(F32) + after_ref[...].astype(F32)).astype(BF)
    second = dot(back, hidden_ref[...], (1, 0))
    hidden_grad = dot(back, w2_ref[...], (0, 0))
    pre_grad = (hidden_grad * slope_ref[...]).astype(BF)
    first = dot(summed_ref[...], pre_grad, (0, 0))
    out_ref[pl.ds(0, feats), :] = first.astype(BF)
    out_ref[pl.ds(feats, classes), :] = second.astype(BF)
    rest = out_ref.shape[0] - feats - classes
    if rest:
        out_ref[pl.ds(feats + classes, rest), :] = jnp.zeros((rest, out_ref.shape[1]), BF)


def logits_kernel(slab_ref, before_ref, own_ref, after_ref, out_ref):
    rows = slab_ref.shape[0]
    total = dot(before_ref[...], slab_ref[:, pl.ds(0, rows)], (1, 1))
    total += dot(own_ref[...], slab_ref[:, pl.ds(rows, rows)], (1, 1))
    total += dot(after_ref[...], slab_ref[:, pl.ds(2 * rows, rows)], (1, 1))
    out_ref[...] = total.astype(out_ref.dtype)


def sum_kernel(parts_ref, out_ref):
    total = parts_ref[0].astype(F32)
    for i in range(1, parts_ref.shape[0]):
        total += parts_ref[i].astype(F32)
    total = total.astype(BF)
    for i in range(out_ref.shape[0]):
        out_ref[i] = total


def unpack_kernel(whole_ref, first_ref, second_ref):
    feats, classes = first_ref.shape[0], second_ref.shape[0]
    first_ref[...] = whole_ref[pl.ds(0, feats), :].astype(F32)
    second_ref[...] = whole_ref[pl.ds(feats, classes), :].astype(F32)


def to_chunks(x, chunks):
    rows, width = x.shape
    return x.reshape(rows // 8, 8, width // TILE, TILE).transpose(0, 2, 1, 3).reshape(chunks, -1, TILE)


def from_chunks(x, width):
    return x.reshape(-1, width // TILE, 8, TILE).transpose(0, 2, 1, 3).reshape(-1, width)


def summed_everywhere(x):
    panels, reps = lax.axis_size("rows"), lax.axis_size("rep")
    devices, layers = panels * reps, 8
    plane = devices // layers
    planes = [[b * plane + i for i in range(plane)] for b in range(layers)]
    columns = [[b * plane + i for b in range(layers)] for i in range(plane)]
    exchange = lambda v, groups: lax.all_to_all(v, ("rows", "rep"), 0, 0, axis_index_groups=groups)
    chunks = to_chunks(x, plane)
    chunk = chunks.shape[1:]
    (copies,) = call(sum_kernel, [jax.ShapeDtypeStruct((layers, *chunk), BF)], [exchange(chunks, planes)])
    (copies,) = call(sum_kernel, [jax.ShapeDtypeStruct((plane, *chunk), BF)], [exchange(copies, columns)])
    return from_chunks(exchange(copies, planes), x.shape[1])


def body(features, w_first, w_second, adj_blocks, adj_cols, train_mask, cotangent):
    panels, reps = lax.axis_size("rows"), lax.axis_size("rep")
    rows, feats = features.shape
    block_rows = adj_cols.shape[2]
    hidden_units, classes = w_second.shape
    up = [(i, (i + 1) % panels) for i in range(panels)]
    down = [(j, i) for i, j in up]
    swap = [(i, (i + 1) % reps) for i in range(reps)]
    shape = jax.ShapeDtypeStruct
    w2 = w_second.T
    cot = cotangent.T

    feats_before = lax.ppermute(features, "rows", up)
    feats_after = lax.ppermute(features, "rows", down)
    first = ((lax.axis_index("rows") - 1) * block_rows).astype(jnp.int32).reshape(1)
    tiles = pltpu.with_memory_space_constraint(adj_blocks[0], pltpu.HBM)
    columns = pltpu.with_memory_space_constraint(adj_cols[0].T, pltpu.HBM)
    (slab,) = call(
        slab_kernel,
        [shape((rows, 3 * rows), BF)],
        [first, columns, tiles],
        [
            pltpu.VMEM((rows, 3 * rows), F32),
            pltpu.SMEM(columns.shape, columns.dtype),
            pltpu.VMEM(tiles.shape, tiles.dtype),
            pltpu.SemaphoreType.DMA((tiles.shape[0] + 1,)),
        ],
        flops=6 * rows * rows,
        specs=[SMEM, ANY, ANY],
    )

    (mine,) = call(
        first_sum_kernel, [shape((rows, feats), BF)], [slab, feats_before, features, feats_after], flops=6 * rows * rows * feats
    )
    other = lax.ppermute(mine, "rep", swap)
    to_before, own, to_after = call(
        back_kernel,
        [shape((classes, rows), BF), shape((classes, rows), F32), shape((classes, rows), BF)],
        [slab, cot, train_mask.reshape(1, rows), mine],
        flops=10**10,
        specs=[VMEM, VMEM, VMEM, ANY],
    )
    back_after = lax.ppermute(to_before, "rows", down)
    back_before = lax.ppermute(to_after, "rows", up)
    summed, hidden, slope, proj = call(
        hidden_kernel,
        [shape((rows, feats), BF), shape((rows, hidden_units), BF), shape((rows, hidden_units), F32), shape((classes, rows), BF)],
        [mine, other, w_first, w2],
        flops=10**10,
    )
    proj_before = lax.ppermute(proj, "rows", up)
    proj_after = lax.ppermute(proj, "rows", down)

    tile_rows = 8 * 8
    padded = -(-(feats + classes) // tile_rows) * tile_rows
    (grads,) = call(
        grads_kernel,
        [shape((padded, hidden_units), BF)],
        [summed, hidden, slope, own, back_before, back_after, w2],
        flops=2 * rows * hidden_units * (feats + 2 * classes),
    )
    grad_first, grad_second = call(
        unpack_kernel, [shape((feats, hidden_units), F32), shape((classes, hidden_units), F32)], [summed_everywhere(grads)]
    )
    grad_second = grad_second.T

    (mine_logits,) = call(
        logits_kernel, [shape((classes, rows), BF)], [slab, proj_before, proj, proj_after], flops=6 * rows * rows * classes
    )
    other_logits = lax.ppermute(mine_logits, "rep", swap)
    logits = (mine_logits.astype(F32) + other_logits.astype(F32)).astype(BF).T
    return (logits, grad_first, grad_second)


def solution(mesh):
    in_specs = (
        P("rows", None),
        P(),
        P(),
        P("rows", "rep", None, None, None),
        P("rows", "rep", None),
        P("rows"),
        P("rows", None),
    )
    out_specs = (P("rows", None), P(), P())
    return jax.shard_map(body, mesh=mesh, in_specs=in_specs, out_specs=out_specs, check_vma=False)
```

```python
import jax
import jax.numpy as jnp
from jax import lax
from jax.experimental import pallas as pl
from jax.experimental.pallas import tpu as pltpu
from jax.sharding import PartitionSpec as P

BF = jnp.bfloat16
F32 = jnp.float32
TILE = 128
ROOT = 0.7978845608028654
CUBE = 0.044715
VMEM = pl.BlockSpec(memory_space=pltpu.VMEM)
ANY = pl.BlockSpec(memory_space=pl.ANY)
SMEM = pl.BlockSpec(memory_space=pltpu.SMEM)


def dot(a, b, contract):
    return lax.dot_general(a, b, ((contract[:1], contract[1:]), ((), ())), preferred_element_type=F32)


def call(kernel, outs, ins, scratch=(), flops=0, specs=None, vmem=48 * 2**20):
    size = lambda x: x.size * x.dtype.itemsize
    moved = sum(map(size, ins)) + sum(map(size, outs))
    return pl.pallas_call(
        kernel,
        out_shape=outs,
        in_specs=specs or [VMEM] * len(ins),
        out_specs=[VMEM] * len(outs),
        scratch_shapes=list(scratch),
        compiler_params=pltpu.CompilerParams(vmem_limit_bytes=vmem),
        cost_estimate=pl.CostEstimate(flops=flops, bytes_accessed=moved, transcendentals=0),
    )(*ins)


def slab_kernel(first_ref, cols_hbm, blocks_hbm, slab_ref, acc, cols_ref, blocks_ref, sems):
    slots, block_rows = blocks_ref.shape[:2]
    copies = [pltpu.make_async_copy(cols_hbm, cols_ref, sems.at[slots])]
    copies += [pltpu.make_async_copy(blocks_hbm.at[k], blocks_ref.at[k], sems.at[k]) for k in range(slots)]
    for copy in copies:
        copy.start()
    first = first_ref[0]
    acc[...] = jnp.zeros_like(acc)
    copies[0].wait()
    for k in range(slots):
        copies[1 + k].wait()
        for r in range(block_rows):
            local = cols_ref[r, k] - first
            where = (pl.ds(r * TILE, TILE), pl.ds(pl.multiple_of(local * TILE, TILE), TILE))
            acc[where] += blocks_ref[k, r].astype(F32)
    slab_ref[...] = acc[...].astype(BF)


def back_kernel(slab_ref, cot_ref, mask_ref, to_before_ref, own_ref, to_after_ref):
    rows = slab_ref.shape[0]
    grad = cot_ref[...] * mask_ref[...].astype(BF)
    for part, out in enumerate((to_before_ref, own_ref, to_after_ref)):
        out[...] = dot(grad, slab_ref[:, pl.ds(part * rows, rows)], (1, 0)).astype(out.dtype)


def first_sum_kernel(slab_ref, before_ref, own_ref, after_ref, out_ref):
    rows = slab_ref.shape[0]
    total = dot(slab_ref[:, pl.ds(0, rows)], before_ref[...], (1, 0))
    total += dot(slab_ref[:, pl.ds(rows, rows)], own_ref[...], (1, 0))
    total += dot(slab_ref[:, pl.ds(2 * rows, rows)], after_ref[...], (1, 0))
    out_ref[...] = total.astype(out_ref.dtype)


def dense_kernel(mine_ref, other_ref, w1_ref, w2_ref, own_ref, before_ref, after_ref, proj_ref, out_ref, hidden_ref, summed_ref, pre_ref):
    rows, feats = mine_ref.shape
    classes = own_ref.shape[0]
    back = (own_ref[...] + before_ref[...].astype(F32) + after_ref[...].astype(F32)).astype(BF)
    for start in range(0, rows, TILE):
        here = pl.ds(start, TILE)
        summed = (mine_ref[here, :].astype(F32) + other_ref[here, :].astype(F32)).astype(BF)
        summed_ref[here, :] = summed
        hidden_grad = dot(back[:, start : start + TILE], w2_ref[...], (0, 0))
        v = dot(summed, w1_ref[...], (1, 0))
        square = v * v
        t = jnp.tanh(ROOT * (v + CUBE * (square * v)))
        half = 0.5 * (1.0 + t)
        hidden = (v * half).astype(BF)
        hidden_ref[here, :] = hidden
        slope = half + (0.5 * ROOT) * v * ((1.0 - t) * (1.0 + t)) * (1.0 + (3.0 * CUBE) * square)
        pre_ref[here, :] = (hidden_grad * slope).astype(BF)
        proj_ref[:, here] = dot(w2_ref[...], hidden, (1, 1)).astype(BF)
    out_ref[pl.ds(0, feats), :] = dot(summed_ref[...], pre_ref[...], (0, 0)).astype(BF)
    out_ref[pl.ds(feats, classes), :] = dot(back, hidden_ref[...], (1, 0)).astype(BF)
    rest = out_ref.shape[0] - feats - classes
    if rest:
        out_ref[pl.ds(feats + classes, rest), :] = jnp.zeros((rest, out_ref.shape[1]), BF)


def logits_kernel(slab_ref, before_ref, own_ref, after_ref, out_ref):
    rows = slab_ref.shape[0]
    total = dot(before_ref[...], slab_ref[:, pl.ds(0, rows)], (1, 1))
    total += dot(own_ref[...], slab_ref[:, pl.ds(rows, rows)], (1, 1))
    total += dot(after_ref[...], slab_ref[:, pl.ds(2 * rows, rows)], (1, 1))
    out_ref[...] = total.astype(out_ref.dtype)


def sum_kernel(parts_ref, out_ref):
    total = parts_ref[0].astype(F32)
    for i in range(1, parts_ref.shape[0]):
        total += parts_ref[i].astype(F32)
    total = total.astype(BF)
    for i in range(out_ref.shape[0]):
        out_ref[i] = total


def unpack_kernel(whole_ref, first_ref, second_ref):
    feats, classes = first_ref.shape[0], second_ref.shape[0]
    first_ref[...] = whole_ref[pl.ds(0, feats), :].astype(F32)
    second_ref[...] = whole_ref[pl.ds(feats, classes), :].astype(F32)


def to_chunks(x, chunks):
    rows, width = x.shape
    return x.reshape(rows // 8, 8, width // TILE, TILE).transpose(0, 2, 1, 3).reshape(chunks, -1, TILE)


def from_chunks(x, width):
    return x.reshape(-1, width // TILE, 8, TILE).transpose(0, 2, 1, 3).reshape(-1, width)


def summed_everywhere(x):
    panels, reps = lax.axis_size("rows"), lax.axis_size("rep")
    devices, layers = panels * reps, 8
    plane = devices // layers
    planes = [[b * plane + i for i in range(plane)] for b in range(layers)]
    columns = [[b * plane + i for b in range(layers)] for i in range(plane)]
    exchange = lambda v, groups: lax.all_to_all(v, ("rows", "rep"), 0, 0, axis_index_groups=groups)
    chunks = to_chunks(x, plane)
    chunk = chunks.shape[1:]
    (copies,) = call(sum_kernel, [jax.ShapeDtypeStruct((layers, *chunk), BF)], [exchange(chunks, planes)])
    (copies,) = call(sum_kernel, [jax.ShapeDtypeStruct((plane, *chunk), BF)], [exchange(copies, columns)])
    return from_chunks(exchange(copies, planes), x.shape[1])


def body(features, w_first, w_second, adj_blocks, adj_cols, train_mask, cotangent):
    panels, reps = lax.axis_size("rows"), lax.axis_size("rep")
    rows, feats = features.shape
    block_rows = adj_cols.shape[2]
    hidden_units, classes = w_second.shape
    up = [(i, (i + 1) % panels) for i in range(panels)]
    down = [(j, i) for i, j in up]
    swap = [(i, (i + 1) % reps) for i in range(reps)]
    shape = jax.ShapeDtypeStruct
    w2 = w_second.T
    cot = cotangent.T

    feats_before = lax.ppermute(features, "rows", up)
    feats_after = lax.ppermute(features, "rows", down)
    first = ((lax.axis_index("rows") - 1) * block_rows).astype(jnp.int32).reshape(1)
    tiles = pltpu.with_memory_space_constraint(adj_blocks[0], pltpu.HBM)
    columns = pltpu.with_memory_space_constraint(adj_cols[0].T, pltpu.HBM)
    (slab,) = call(
        slab_kernel,
        [shape((rows, 3 * rows), BF)],
        [first, columns, tiles],
        [
            pltpu.VMEM((rows, 3 * rows), F32),
            pltpu.SMEM(columns.shape, columns.dtype),
            pltpu.VMEM(tiles.shape, tiles.dtype),
            pltpu.SemaphoreType.DMA((tiles.shape[0] + 1,)),
        ],
        flops=6 * rows * rows,
        specs=[SMEM, ANY, ANY],
    )

    to_before, own, to_after = call(
        back_kernel,
        [shape((classes, rows), BF), shape((classes, rows), F32), shape((classes, rows), BF)],
        [slab, cot, train_mask.reshape(1, rows)],
        flops=10**6,
        specs=[VMEM, VMEM, VMEM],
    )
    back_after = lax.ppermute(to_before, "rows", down)
    back_before = lax.ppermute(to_after, "rows", up)
    (mine,) = call(
        first_sum_kernel, [shape((rows, feats), BF)], [slab, feats_before, features, feats_after], flops=6 * rows * rows * feats
    )
    other = lax.ppermute(mine, "rep", swap)
    tile_rows = 8 * 8
    padded = -(-(feats + classes) // tile_rows) * tile_rows
    proj, grads = call(
        dense_kernel,
        [shape((classes, rows), BF), shape((padded, hidden_units), BF)],
        [mine, other, w_first, w2, own, back_before, back_after],
        [pltpu.VMEM((rows, hidden_units), BF), pltpu.VMEM((rows, feats), BF), pltpu.VMEM((rows, hidden_units), BF)],
        flops=4 * rows * hidden_units * (feats + 2 * classes),
    )
    proj_before = lax.ppermute(proj, "rows", up)
    proj_after = lax.ppermute(proj, "rows", down)

    grad_first, grad_second = call(
        unpack_kernel, [shape((feats, hidden_units), F32), shape((classes, hidden_units), F32)], [summed_everywhere(grads)]
    )
    grad_second = grad_second.T

    (mine_logits,) = call(
        logits_kernel, [shape((classes, rows), BF)], [slab, proj_before, proj, proj_after], flops=6 * rows * rows * classes
    )
    other_logits = lax.ppermute(mine_logits, "rep", swap)
    logits = (mine_logits.astype(F32) + other_logits.astype(F32)).astype(BF).T
    return (logits, grad_first, grad_second)


def solution(mesh):
    in_specs = (
        P("rows", None),
        P(),
        P(),
        P("rows", "rep", None, None, None),
        P("rows", "rep", None),
        P("rows"),
        P("rows", None),
    )
    out_specs = (P("rows", None), P(), P())
    return jax.shard_map(body, mesh=mesh, in_specs=in_specs, out_specs=out_specs, check_vma=False)
```

```python
import jax
import jax.numpy as jnp
from jax import lax
from jax.experimental import pallas as pl
from jax.experimental.pallas import tpu as pltpu
from jax.sharding import PartitionSpec as P

BF = jnp.bfloat16
F32 = jnp.float32
TILE = 128
ROOT = 0.7978845608028654
CUBE = 0.044715
VMEM = pl.BlockSpec(memory_space=pltpu.VMEM)
ANY = pl.BlockSpec(memory_space=pl.ANY)


def dot(a, b, contract):
    return lax.dot_general(a, b, ((contract[:1], contract[1:]), ((), ())), preferred_element_type=F32)


def call(kernel, outs, ins, scratch=(), flops=0, specs=None, vmem=48 * 2**20):
    size = lambda x: x.size * x.dtype.itemsize
    moved = sum(map(size, ins)) + sum(map(size, outs))
    return pl.pallas_call(
        kernel,
        out_shape=outs,
        in_specs=specs or [VMEM] * len(ins),
        out_specs=[VMEM] * len(outs),
        scratch_shapes=list(scratch),
        compiler_params=pltpu.CompilerParams(vmem_limit_bytes=vmem),
        cost_estimate=pl.CostEstimate(flops=flops, bytes_accessed=moved, transcendentals=0),
    )(*ins)


def slab_kernel( cols_hbm, blocks_hbm, slab_ref, acc, cols_ref, blocks_ref, sems):
    slots, block_rows = blocks_ref.shape[:2]
    copies = [pltpu.make_async_copy(cols_hbm, cols_ref, sems.at[slots])]
    copies += [pltpu.make_async_copy(blocks_hbm.at[k], blocks_ref.at[k], sems.at[k]) for k in range(slots)]
    for copy in copies:
        copy.start()
    first = (lax.axis_index("rows") - 1) * block_rows
    acc[...] = jnp.zeros_like(acc)
    copies[0].wait()
    for k in range(slots):
        copies[1 + k].wait()
        for r in range(block_rows):
            local = cols_ref[r, k] - first
            where = (pl.ds(r * TILE, TILE), pl.ds(pl.multiple_of(local * TILE, TILE), TILE))
            acc[where] += blocks_ref[k, r].astype(F32)
    slab_ref[...] = acc[...].astype(BF)


def parts_of(slab_ref):
    rows = slab_ref.shape[0]
    odd = lax.axis_index("rows") % 2
    starts = ((1 - odd) * (2 * rows), rows, odd * (2 * rows))
    return [slab_ref[:, pl.ds(pl.multiple_of(start, TILE), rows)] for start in starts]


def back_kernel(slab_ref, cot_ref, mask_ref, near_ref, own_ref, far_ref):
    grad = cot_ref[...] * mask_ref[...].astype(BF)
    for part, out in zip(parts_of(slab_ref), (near_ref, own_ref, far_ref)):
        out[...] = dot(grad, part, (1, 0)).astype(out.dtype)


def first_sum_kernel(slab_ref, near_ref, own_ref, far_ref, out_ref):
    near, own, far = parts_of(slab_ref)
    total = dot(near, near_ref[...], (1, 0)) + dot(own, own_ref[...], (1, 0)) + dot(far, far_ref[...], (1, 0))
    out_ref[...] = total.astype(out_ref.dtype)


def dense_kernel(mine_ref, other_ref, w1_ref, w2_ref, own_ref, near_ref, far_ref, proj_ref, out_ref, hidden_ref, summed_ref, pre_ref):
    rows, feats = mine_ref.shape
    classes = own_ref.shape[0]
    back = (own_ref[...] + near_ref[...].astype(F32) + far_ref[...].astype(F32)).astype(BF)
    for start in range(0, rows, TILE):
        here = pl.ds(start, TILE)
        summed = (mine_ref[here, :].astype(F32) + other_ref[here, :].astype(F32)).astype(BF)
        summed_ref[here, :] = summed
        hidden_grad = dot(back[:, start : start + TILE], w2_ref[...], (0, 0))
        v = dot(summed, w1_ref[...], (1, 0))
        square = v * v
        t = jnp.tanh(ROOT * (v + CUBE * (square * v)))
        half = 0.5 * (1.0 + t)
        hidden = (v * half).astype(BF)
        hidden_ref[here, :] = hidden
        slope = half + (0.5 * ROOT) * v * ((1.0 - t) * (1.0 + t)) * (1.0 + (3.0 * CUBE) * square)
        pre_ref[here, :] = (hidden_grad * slope).astype(BF)
        proj_ref[:, here] = dot(w2_ref[...], hidden, (1, 1)).astype(BF)
    out_ref[pl.ds(0, feats), :] = dot(summed_ref[...], pre_ref[...], (0, 0)).astype(BF)
    out_ref[pl.ds(feats, classes), :] = dot(back, hidden_ref[...], (1, 0)).astype(BF)
    rest = out_ref.shape[0] - feats - classes
    if rest:
        out_ref[pl.ds(feats + classes, rest), :] = jnp.zeros((rest, out_ref.shape[1]), BF)


def logits_kernel(slab_ref, near_ref, own_ref, far_ref, out_ref):
    near, own, far = parts_of(slab_ref)
    total = dot(near_ref[...], near, (1, 1)) + dot(own_ref[...], own, (1, 1)) + dot(far_ref[...], far, (1, 1))
    out_ref[...] = total.astype(out_ref.dtype)


def sum_kernel(parts_ref, out_ref):
    total = parts_ref[0].astype(F32)
    for i in range(1, parts_ref.shape[0]):
        total += parts_ref[i].astype(F32)
    total = total.astype(BF)
    for i in range(out_ref.shape[0]):
        out_ref[i] = total


def unpack_kernel(whole_ref, first_ref, second_ref):
    feats, classes = first_ref.shape[0], second_ref.shape[0]
    first_ref[...] = whole_ref[pl.ds(0, feats), :].astype(F32)
    second_ref[...] = whole_ref[pl.ds(feats, classes), :].astype(F32)


def to_chunks(x, chunks):
    rows, width = x.shape
    return x.reshape(rows // 8, 8, width // TILE, TILE).transpose(0, 2, 1, 3).reshape(chunks, -1, TILE)


def from_chunks(x, width):
    return x.reshape(-1, width // TILE, 8, TILE).transpose(0, 2, 1, 3).reshape(-1, width)


def summed_everywhere(x):
    panels, reps = lax.axis_size("rows"), lax.axis_size("rep")
    devices, layers = panels * reps, 8
    plane = devices // layers
    planes = [[b * plane + i for i in range(plane)] for b in range(layers)]
    columns = [[b * plane + i for b in range(layers)] for i in range(plane)]
    exchange = lambda v, groups: lax.all_to_all(v, ("rows", "rep"), 0, 0, axis_index_groups=groups)
    chunks = to_chunks(x, plane)
    chunk = chunks.shape[1:]
    (copies,) = call(sum_kernel, [jax.ShapeDtypeStruct((layers, *chunk), BF)], [exchange(chunks, planes)])
    (copies,) = call(sum_kernel, [jax.ShapeDtypeStruct((plane, *chunk), BF)], [exchange(copies, columns)])
    return from_chunks(exchange(copies, planes), x.shape[1])


def body(features, w_first, w_second, adj_blocks, adj_cols, train_mask, cotangent):
    panels, reps = lax.axis_size("rows"), lax.axis_size("rep")
    rows, feats = features.shape
    block_rows = adj_cols.shape[2]
    hidden_units, classes = w_second.shape
    near = [(i, i ^ 1) for i in range(panels)]
    far = [(i, (i + (1 if i % 2 else -1)) % panels) for i in range(panels)]
    swap = [(i, (i + 1) % reps) for i in range(reps)]
    shape = jax.ShapeDtypeStruct
    w2 = w_second.T
    cot = cotangent.T

    feats_far = lax.ppermute(features, "rows", far)
    feats_near = lax.ppermute(features, "rows", near)
    tiles = pltpu.with_memory_space_constraint(adj_blocks[0], pltpu.HBM)
    columns = pltpu.with_memory_space_constraint(adj_cols[0].T, pltpu.HBM)
    (slab,) = call(
        slab_kernel,
        [shape((rows, 3 * rows), BF)],
        [columns, tiles],
        [
            pltpu.VMEM((rows, 3 * rows), F32),
            pltpu.SMEM(columns.shape, columns.dtype),
            pltpu.VMEM(tiles.shape, tiles.dtype),
            pltpu.SemaphoreType.DMA((tiles.shape[0] + 1,)),
        ],
        flops=6 * rows * rows,
        specs=[ANY, ANY],
    )

    to_near, own, to_far = call(
        back_kernel,
        [shape((classes, rows), BF), shape((classes, rows), F32), shape((classes, rows), BF)],
        [slab, cot, train_mask.reshape(1, rows)],
        flops=10**6,
    )
    back_far = lax.ppermute(to_far, "rows", far)
    back_near = lax.ppermute(to_near, "rows", near)
    (mine,) = call(
        first_sum_kernel,
        [shape((rows, feats), BF)],
        [slab, feats_near, features, feats_far],
        flops=6 * rows * rows * feats,
    )
    other = lax.ppermute(mine, "rep", swap)
    tile_rows = 8 * 8
    padded = -(-(feats + classes) // tile_rows) * tile_rows
    proj, grads = call(
        dense_kernel,
        [shape((classes, rows), BF), shape((padded, hidden_units), BF)],
        [mine, other, w_first, w2, own, back_near, back_far],
        [pltpu.VMEM((rows, hidden_units), BF), pltpu.VMEM((rows, feats), BF), pltpu.VMEM((rows, hidden_units), BF)],
        flops=4 * rows * hidden_units * (feats + 2 * classes),
    )
    proj_far = lax.ppermute(proj, "rows", far)
    proj_near = lax.ppermute(proj, "rows", near)

    grad_first, grad_second = call(
        unpack_kernel, [shape((feats, hidden_units), F32), shape((classes, hidden_units), F32)], [summed_everywhere(grads)]
    )
    grad_second = grad_second.T

    (mine_logits,) = call(
        logits_kernel,
        [shape((classes, rows), BF)],
        [slab, proj_near, proj, proj_far],
        flops=6 * rows * rows * classes,
    )
    other_logits = lax.ppermute(mine_logits, "rep", swap)
    logits = (mine_logits.astype(F32) + other_logits.astype(F32)).astype(BF).T
    return (logits, grad_first, grad_second)


def solution(mesh):
    in_specs = (
        P("rows", None),
        P(),
        P(),
        P("rows", "rep", None, None, None),
        P("rows", "rep", None),
        P("rows"),
        P("rows", None),
    )
    out_specs = (P("rows", None), P(), P())
    return jax.shard_map(body, mesh=mesh, in_specs=in_specs, out_specs=out_specs, check_vma=False)
```

```python
import jax
import jax.numpy as jnp
from jax import lax
from jax.experimental import pallas as pl
from jax.experimental.pallas import tpu as pltpu
from jax.sharding import PartitionSpec as P

BF = jnp.bfloat16
F32 = jnp.float32
TILE = 128
ROOT = 0.7978845608028654
CUBE = 0.044715
VMEM = pl.BlockSpec(memory_space=pltpu.VMEM)
ANY = pl.BlockSpec(memory_space=pl.ANY)


def dot(a, b, contract):
    return lax.dot_general(a, b, ((contract[:1], contract[1:]), ((), ())), preferred_element_type=F32)


def call(kernel, outs, ins, scratch=(), flops=0, specs=None, out_specs=None, vmem=48 * 2**20):
    size = lambda x: x.size * x.dtype.itemsize
    moved = sum(map(size, ins)) + sum(map(size, outs))
    return pl.pallas_call(
        kernel,
        out_shape=outs,
        in_specs=specs or [VMEM] * len(ins),
        out_specs=out_specs or [VMEM] * len(outs),
        scratch_shapes=list(scratch),
        compiler_params=pltpu.CompilerParams(vmem_limit_bytes=vmem),
        cost_estimate=pl.CostEstimate(flops=flops, bytes_accessed=moved, transcendentals=0),
    )(*ins)


def slab_kernel( cols_hbm, blocks_hbm, slab_ref, acc, cols_ref, blocks_ref, sems):
    slots, block_rows = blocks_ref.shape[:2]
    copies = [pltpu.make_async_copy(cols_hbm, cols_ref, sems.at[slots])]
    copies += [pltpu.make_async_copy(blocks_hbm.at[k], blocks_ref.at[k], sems.at[k]) for k in range(slots)]
    for copy in copies:
        copy.start()
    first = (lax.axis_index("rows") - 1) * block_rows
    acc[...] = jnp.zeros_like(acc)
    copies[0].wait()
    for k in range(slots):
        copies[1 + k].wait()
        for r in range(block_rows):
            local = cols_ref[r, k] - first
            where = (pl.ds(r * TILE, TILE), pl.ds(pl.multiple_of(local * TILE, TILE), TILE))
            acc[where] += blocks_ref[k, r].astype(F32)
    slab_ref[...] = acc[...].astype(BF)


def parts_of(slab_ref):
    rows = slab_ref.shape[0]
    odd = lax.axis_index("rows") % 2
    starts = ((1 - odd) * (2 * rows), rows, odd * (2 * rows))
    return [slab_ref[:, pl.ds(pl.multiple_of(start, TILE), rows)] for start in starts]


def back_kernel(slab_ref, cot_ref, mask_ref, feats_ref, near_ref, own_ref, far_ref, partial_ref):
    grad = cot_ref[...] * mask_ref[...].astype(BF)
    for part, out in zip(parts_of(slab_ref), (near_ref, own_ref, far_ref)):
        out[...] = dot(grad, part, (1, 0)).astype(out.dtype)
    rows = slab_ref.shape[0]
    partial_ref[...] = dot(slab_ref[:, pl.ds(rows, rows)], feats_ref[...], (1, 0))


def first_sum_kernel(slab_ref, near_ref, partial_ref, far_ref, out_ref):
    near, _, far = parts_of(slab_ref)
    total = dot(near, near_ref[...], (1, 0)) + partial_ref[...] + dot(far, far_ref[...], (1, 0))
    out_ref[...] = total.astype(out_ref.dtype)


def dense_kernel(mine_ref, other_ref, w1_ref, w2_ref, own_ref, near_ref, far_ref, proj_ref, out_ref, hidden_ref, summed_ref, pre_ref):
    rows, feats = mine_ref.shape
    classes = own_ref.shape[0]
    back = (own_ref[...] + near_ref[...].astype(F32) + far_ref[...].astype(F32)).astype(BF)
    for start in range(0, rows, TILE):
        here = pl.ds(start, TILE)
        summed = (mine_ref[here, :].astype(F32) + other_ref[here, :].astype(F32)).astype(BF)
        summed_ref[here, :] = summed
        hidden_grad = dot(back[:, start : start + TILE], w2_ref[...], (0, 0))
        v = dot(summed, w1_ref[...], (1, 0))
        square = v * v
        t = jnp.tanh(ROOT * (v + CUBE * (square * v)))
        half = 0.5 * (1.0 + t)
        hidden = (v * half).astype(BF)
        hidden_ref[here, :] = hidden
        slope = half + (0.5 * ROOT) * v * ((1.0 - t) * (1.0 + t)) * (1.0 + (3.0 * CUBE) * square)
        pre_ref[here, :] = (hidden_grad * slope).astype(BF)
        proj_ref[:, here] = dot(w2_ref[...], hidden, (1, 1)).astype(BF)
    out_ref[pl.ds(0, feats), :] = dot(summed_ref[...], pre_ref[...], (0, 0)).astype(BF)
    out_ref[pl.ds(feats, classes), :] = dot(back, hidden_ref[...], (1, 0)).astype(BF)
    rest = out_ref.shape[0] - feats - classes
    if rest:
        out_ref[pl.ds(feats + classes, rest), :] = jnp.zeros((rest, out_ref.shape[1]), BF)


def logits_kernel(slab_ref, near_ref, own_ref, far_ref, out_ref):
    near, own, far = parts_of(slab_ref)
    total = dot(near_ref[...], near, (1, 1)) + dot(own_ref[...], own, (1, 1)) + dot(far_ref[...], far, (1, 1))
    out_ref[...] = total.astype(out_ref.dtype)


def sum_kernel(parts_ref, out_ref):
    total = parts_ref[0].astype(F32)
    for i in range(1, parts_ref.shape[0]):
        total += parts_ref[i].astype(F32)
    total = total.astype(BF)
    for i in range(out_ref.shape[0]):
        out_ref[i] = total


def unpack_kernel(whole_ref, first_out, second_out, first_ref, second_ref, sems):
    feats, classes = first_ref.shape[0], second_ref.shape[0]
    second_ref[...] = whole_ref[pl.ds(feats, classes), :].astype(F32)
    second_copy = pltpu.make_async_copy(second_ref, second_out, sems.at[0])
    second_copy.start()
    first_ref[...] = whole_ref[pl.ds(0, feats), :].astype(F32)
    first_copy = pltpu.make_async_copy(first_ref, first_out, sems.at[1])
    first_copy.start()
    second_copy.wait()
    first_copy.wait()


def to_chunks(x, chunks):
    rows, width = x.shape
    return x.reshape(rows // 8, 8, width // TILE, TILE).transpose(0, 2, 1, 3).reshape(chunks, -1, TILE)


def from_chunks(x, width):
    return x.reshape(-1, width // TILE, 8, TILE).transpose(0, 2, 1, 3).reshape(-1, width)


def summed_everywhere(x):
    panels, reps = lax.axis_size("rows"), lax.axis_size("rep")
    devices, layers = panels * reps, 8
    plane = devices // layers
    planes = [[b * plane + i for i in range(plane)] for b in range(layers)]
    columns = [[b * plane + i for b in range(layers)] for i in range(plane)]
    exchange = lambda v, groups: lax.all_to_all(v, ("rows", "rep"), 0, 0, axis_index_groups=groups)
    chunks = to_chunks(x, plane)
    chunk = chunks.shape[1:]
    (copies,) = call(sum_kernel, [jax.ShapeDtypeStruct((layers, *chunk), BF)], [exchange(chunks, planes)])
    (copies,) = call(sum_kernel, [jax.ShapeDtypeStruct((plane, *chunk), BF)], [exchange(copies, columns)])
    return from_chunks(exchange(copies, planes), x.shape[1])


def body(features, w_first, w_second, adj_blocks, adj_cols, train_mask, cotangent):
    panels, reps = lax.axis_size("rows"), lax.axis_size("rep")
    rows, feats = features.shape
    block_rows = adj_cols.shape[2]
    hidden_units, classes = w_second.shape
    near = [(i, i ^ 1) for i in range(panels)]
    far = [(i, (i + (1 if i % 2 else -1)) % panels) for i in range(panels)]
    swap = [(i, (i + 1) % reps) for i in range(reps)]
    shape = jax.ShapeDtypeStruct
    w2 = w_second.T
    cot = cotangent.T

    feats_far = lax.ppermute(features, "rows", far)
    feats_near = lax.ppermute(features, "rows", near)
    tiles = pltpu.with_memory_space_constraint(adj_blocks[0], pltpu.HBM)
    columns = pltpu.with_memory_space_constraint(adj_cols[0].T, pltpu.HBM)
    (slab,) = call(
        slab_kernel,
        [shape((rows, 3 * rows), BF)],
        [columns, tiles],
        [
            pltpu.VMEM((rows, 3 * rows), F32),
            pltpu.SMEM(columns.shape, columns.dtype),
            pltpu.VMEM(tiles.shape, tiles.dtype),
            pltpu.SemaphoreType.DMA((tiles.shape[0] + 1,)),
        ],
        flops=6 * rows * rows,
        specs=[ANY, ANY],
    )

    to_near, own, to_far, partial = call(
        back_kernel,
        [shape((classes, rows), BF), shape((classes, rows), F32), shape((classes, rows), BF), shape((rows, feats), F32)],
        [slab, cot, train_mask.reshape(1, rows), features],
        flops=10**6,
    )
    back_far = lax.ppermute(to_far, "rows", far)
    back_near = lax.ppermute(to_near, "rows", near)
    (mine,) = call(
        first_sum_kernel,
        [shape((rows, feats), BF)],
        [slab, feats_near, partial, feats_far],
        flops=6 * rows * rows * feats,
    )
    other = lax.ppermute(mine, "rep", swap)
    tile_rows = 8 * 8
    padded = -(-(feats + classes) // tile_rows) * tile_rows
    proj, grads = call(
        dense_kernel,
        [shape((classes, rows), BF), shape((padded, hidden_units), BF)],
        [mine, other, w_first, w2, own, back_near, back_far],
        [pltpu.VMEM((rows, hidden_units), BF), pltpu.VMEM((rows, feats), BF), pltpu.VMEM((rows, hidden_units), BF)],
        flops=4 * rows * hidden_units * (feats + 2 * classes),
    )
    proj_far = lax.ppermute(proj, "rows", far)
    proj_near = lax.ppermute(proj, "rows", near)

    grad_first, grad_second = call(
        unpack_kernel,
        [shape((feats, hidden_units), F32), shape((classes, hidden_units), F32)],
        [summed_everywhere(grads)],
        [pltpu.VMEM((feats, hidden_units), F32), pltpu.VMEM((classes, hidden_units), F32), pltpu.SemaphoreType.DMA((2,))],
        out_specs=[ANY, ANY],
    )
    grad_second = grad_second.T

    (mine_logits,) = call(
        logits_kernel,
        [shape((classes, rows), BF)],
        [slab, proj_near, proj, proj_far],
        flops=6 * rows * rows * classes,
    )
    other_logits = lax.ppermute(mine_logits, "rep", swap)
    logits = (mine_logits.astype(F32) + other_logits.astype(F32)).astype(BF).T
    return (logits, grad_first, grad_second)


def solution(mesh):
    in_specs = (
        P("rows", None),
        P(),
        P(),
        P("rows", "rep", None, None, None),
        P("rows", "rep", None),
        P("rows"),
        P("rows", None),
    )
    out_specs = (P("rows", None), P(), P())
    return jax.shard_map(body, mesh=mesh, in_specs=in_specs, out_specs=out_specs, check_vma=False)
```
